256 devices in a mesh: views: 16 (over x, y), rows: 16 (over z, core).
Axes of the slice: x: 4, y: 4, z: 8, core: 2. Of those that a mesh axis runs over, the one named last changes fastest.
Arguments:
- grad_par: bfloat16 [256, 512, 2048], P('views', None, 'rows'), may hold values from -4 to 12
- contrib_owner: int32 [256, 1], P('views'), may hold values from 0 to 15; in each aligned block of 16 rows (0 to 15, 16 to 31, ...) at most 2 rows name the same one
- contrib_fan: int32 [256], P('views'), may hold values from 0 to 15
- contrib_start: int32 [256], P('views'), may hold values from 0 to 14
- contrib_wt: bfloat16 [256, 2], P('views'), may hold values from 0.19921875 to 1
Outputs:
- fan_grad: bfloat16 [256, 512, 2048], P('views', 'rows')
The draws below stay inside these ranges and needn't reach their ends.
Inputs may be any that keep to these rules, and one draw needn't show every extreme that they name: `contrib_owner`: among the 16 entries of one view group, no owner group is named more than 2 times.
All inputs are finite; a program needn't handle non-finite values.
Results may differ from the reference program's by a relative error of at most 0.001.
The reference program's roundings to bfloat16 on the way count: a program that leaves them out, or rounds other values in their place, can miss the bound.
Values may be sent and summed in bfloat16 or wider, within the bound.
A program may use at most 64 MiB of HBM per device.

```python
import math
import jax
import jax.numpy as jnp
import numpy as np
from jax import lax

C = 2048
PV_DEV = 16
CONTRIB = 16
BAND = 2
CAP = 2
R = 512
PV = 256
FV_DEV = 16
F = 256
N_VIEWS = 16


def draw_grad_par(key, part):
    key = jax.random.fold_in(key, 7)
    k_noise, k_amp, k_half, k_mid = jax.random.split(key, 4)
    row_shape = (PV, R, 1)
    place = jnp.arange(C, dtype=jnp.float32)[None, None, :] + jnp.float32(0.5)
    half_width = jnp.float32(C) * jax.random.uniform(k_half, row_shape, jnp.float32, 0.3, 0.45)
    middle = jnp.float32(C) * (0.5 + jax.random.uniform(k_mid, row_shape, jnp.float32, -0.04, 0.04))
    offset = (place - middle) / half_width
    dome = jnp.sqrt(jnp.maximum(1.0 - offset * offset, 0.0))
    amplitude = jax.random.uniform(k_amp, row_shape, jnp.float32, 3.0, 6.0)
    smooth = amplitude * dome
    noise = jax.random.truncated_normal(k_noise, -4.0, 4.0, (PV, R, C), jnp.float32)
    return (smooth + noise).astype(jnp.bfloat16)


def set_ends(result, stream_key, smallest, high):
    spot = [jax.random.randint(jax.random.fold_in(stream_key, axis), (), 0, length) for axis, length in enumerate(result.shape)]
    main_axis = result.shape.index(max(result.shape))
    beside = spot[:main_axis] + [(spot[main_axis] + 1) % result.shape[main_axis]] + spot[main_axis + 1:]
    return result.at[tuple(spot)].set(smallest).at[tuple(beside)].set(high)


def block_levels(rng, extent, cuts, smallest, top_value):
    loudness = 1.0
    for position, parts in cuts:
        heights = jax.random.uniform(jax.random.fold_in(jax.random.fold_in(rng, 6), position), (parts,), jnp.float32, smallest / len(cuts), top_value / len(cuts))
        loudness = loudness * jnp.repeat(jnp.exp(heights), extent[position] // parts).reshape((-1,) + (1,) * (len(extent) - 1 - position))
    return loudness


def assign_block(own_key, own, number, rows, amount, top, limit, skew):
    ranking = jax.random.permutation(own_key, amount)
    heavy_load, common = load_shares(amount, rows * top, limit, skew, True), load_shares(amount, rows * top, limit, skew, False)
    places = jnp.arange(amount)

    def named(sizes, turn):
        used = int((sizes > 0).sum())
        fixed = max(1, used // 4)
        passed = fixed + (places - fixed + turn * (used - fixed)) % max(1, amount - fixed)
        return jnp.zeros((amount,), jnp.int32).at[ranking[jnp.where(places < fixed, places, passed)]].set(jnp.asarray(sizes, jnp.int32))

    sizes = jnp.where(number % 4 == 0, named(heavy_load, number // 4), named(common, number - number // 4 - 1))
    mixed = jax.random.permutation(jax.random.fold_in(own, 3), amount)
    donor, receiver = mixed[0:amount // 2 * 2:2], mixed[1:amount // 2 * 2:2]
    room = jnp.minimum(sizes[donor] - 1, limit - sizes[receiver]) // 2
    room = jnp.where((donor == ranking[0]) | (receiver == ranking[0]) | (sizes[receiver] == 0), 0, jnp.maximum(room, 0))
    passed = jax.random.randint(jax.random.fold_in(own, 4), (amount // 2,), 0, 1 << 20) % (room + 1)
    sizes = sizes.at[donor].add(-passed).at[receiver].add(passed)
    labels = jnp.searchsorted(jnp.cumsum(sizes), jnp.arange(rows * top), side="right").astype(jnp.int32)
    listing = labels.reshape(top, rows).T
    listing = listing[jax.random.permutation(jax.random.fold_in(own, 1), rows)]
    turn = jax.random.randint(jax.random.fold_in(own, 2), (rows, 1), 0, top)
    return jnp.take_along_axis(listing, (jnp.arange(top)[None, :] + turn) % top, axis=1)


def load_shares(number_of, total, limit, lean, full):
    portions = [(1 << 20) // math.isqrt(grade ** lean) + 1 for grade in range(1, number_of + 1)]
    largest = limit if full else min(limit, max(-(-total // number_of), total * portions[0] // sum(portions)))
    least = 1 if total - largest >= number_of - 1 else 0
    given, rest = [largest] + [least] * (number_of - 1), total - largest - least * (number_of - 1)
    while rest > 0:
        candidates = [i for i in range(1, number_of) if given[i] < largest] or [i for i in range(1, number_of) if given[i] < limit]
        whole, left = sum([portions[i] for i in candidates]), rest
        for i in candidates:
            addition = min(limit - given[i], max(1, left * portions[i] // whole), rest)
            given[i] = given[i] + addition
            rest = rest - addition
    return np.array(given)


def setup_inputs(seed: int = 0) -> dict:
    keys = jax.random.split(jax.random.key(seed), 6)
    grad_par = draw_grad_par(jax.random.fold_in(keys[5], 71), 0)
    contrib_owner_keys = jax.random.split(jax.random.fold_in(keys[1], 1), (N_VIEWS * CONTRIB) // CONTRIB)
    contrib_owner_turns = jax.random.permutation(jax.random.fold_in(keys[1], 3), (N_VIEWS * CONTRIB) // CONTRIB)
    contrib_owner = jax.vmap(lambda own, number: assign_block(jax.random.fold_in(keys[1], 2), own, number, CONTRIB, N_VIEWS, 1, CAP, 2))(contrib_owner_keys, contrib_owner_turns).reshape((N_VIEWS * CONTRIB, 1))
    contrib_fan = set_ends(jax.random.randint(keys[2], (N_VIEWS * CONTRIB,), 0, FV_DEV), jax.random.fold_in(keys[2], 1), 0, FV_DEV - 1).astype(jnp.int32)
    contrib_start = set_ends(jax.random.randint(keys[3], (N_VIEWS * CONTRIB,), 0, PV_DEV - BAND + 1), jax.random.fold_in(keys[3], 1), 0, PV_DEV - BAND).astype(jnp.int32)
    contrib_wt = jnp.clip(0.19921875 + 0.80078125 * jax.random.uniform(keys[4], (N_VIEWS * CONTRIB, BAND), jnp.float32) ** block_levels(keys[4], (N_VIEWS * CONTRIB, BAND), ((0, 16),), -0.2, 0.2), 0.19921875, 1.0).astype(jnp.bfloat16)
    return dict(grad_par=grad_par, contrib_owner=contrib_owner, contrib_fan=contrib_fan, contrib_start=contrib_start, contrib_wt=contrib_wt)


def ramp_matrix(channels):
    positions = lax.iota(jnp.int32, channels)
    distance = jnp.abs(positions[:, None] - positions[None, :])
    far_float = jnp.maximum(distance.astype(jnp.float32), jnp.float32(1.0))
    odd_values = jnp.float32(-4.0) / (jnp.float32(math.pi ** 2) * far_float * far_float)
    values = jnp.where(distance == 0, jnp.float32(1.0), jnp.where(distance % 2 == 1, odd_values, jnp.float32(0.0)))
    return values.astype(jnp.bfloat16)


def reference(grad_par, contrib_owner, contrib_fan, contrib_start, contrib_wt):
    filter_table = ramp_matrix(C).astype(jnp.float32)

    def filter_view(one_view):
        result_rows = jnp.dot(one_view.astype(jnp.float32), filter_table, precision=lax.Precision.HIGHEST)
        return result_rows.astype(jnp.bfloat16)

    filtered = lax.map(filter_view, grad_par)
    total = contrib_owner.shape[0]
    fan_global = (contrib_owner[:, 0].astype(jnp.int32) * FV_DEV + contrib_fan.astype(jnp.int32)).astype(jnp.int32)
    view_base = ((lax.iota(jnp.int32, total) // CONTRIB) * PV_DEV + contrib_start.astype(jnp.int32)).astype(jnp.int32)

    def add_one(index, accumulated):
        index = index.astype(jnp.int32)
        start = view_base[index].astype(jnp.int32)
        band_rows = lax.dynamic_slice_in_dim(filtered, start, BAND, 0).astype(jnp.float32)
        band_weights = contrib_wt[index].astype(jnp.float32)
        contrib = jnp.sum(band_weights[:, None, None] * band_rows, axis=0).astype(jnp.bfloat16)
        contrib = lax.optimization_barrier(contrib).astype(jnp.float32)
        target = fan_global[index].astype(jnp.int32)
        current = lax.dynamic_slice_in_dim(accumulated, target, 1, 0)
        return lax.dynamic_update_slice_in_dim(accumulated, current + contrib[None], target, 0)

    accumulated = lax.fori_loop(jnp.int32(0), jnp.int32(total), add_one, jnp.zeros((F, R, C), jnp.float32))
    return accumulated.astype(jnp.bfloat16)
```

```python
import functools
import math

import jax
import jax.numpy as jnp
import ml_dtypes
import numpy as np
from jax import lax
from jax.experimental import pallas as pl
from jax.experimental.pallas import tpu as pltpu
from jax.sharding import PartitionSpec as P

MESH = pl.DeviceIdType.MESH
BF = jnp.bfloat16
F32 = jnp.float32
I32 = jnp.int32

C = 2048
NV = 16
NR = 16
ROWS = 32
R = 4
N = ROWS // R
FOLD = 16 // R
L = C // FOLD
XY = 4
NZ = 8
LAG = 2

VIEW_OFFS = [(1, 0), (0, 1), (3, 0), (0, 3), (1, 1), (3, 3), (1, 3), (3, 1), (2, 0), (0, 2), (2, 1), (1, 2), (2, 3), (3, 2), (2, 2)]
ROW_OFFS = [(z, c) for z in (1, 7, 2, 6, 3, 5, 4) for c in (0, 1)] + [(0, 1)]


def toeplitz_column():
    m = np.arange(2 * C - 256)[:, None] - np.arange(256)[None, :] - (C - 256)
    distance = np.abs(m)
    far = np.maximum(distance.astype(np.float32), np.float32(1.0))
    odd = np.float32(-4.0) / (np.float32(math.pi**2) * far * far)
    values = np.where(distance == 0, np.float32(1.0), np.where(distance % 2 == 1, odd, np.float32(0.0)))
    return values.astype(ml_dtypes.bfloat16)


def iota(shape, dim):
    return lax.broadcasted_iota(I32, shape, dim)


def wait_for(ref, sem):
    pltpu.make_async_copy(ref, ref, sem).wait()


def kernel(owner_ref, fan_ref, start_ref, wt_ref, x_hbm, g_hbm, out_ref,
           x_in, g, zsrc, zrecv, csrc, fin, raw, msrc, mrecv, wmat, cmat, pmat,
           in_sem, z_send, z_recv, c_send, c_recv, m_send, m_recv):
    v = lax.axis_index("views")
    r = lax.axis_index("rows")
    x, y = v // XY, v % XY
    z, core = r // 2, r % 2

    load_x = pltpu.make_async_copy(x_hbm, x_in, in_sem.at[0])
    load_x.start()
    load_g = pltpu.make_async_copy(g_hbm, g, in_sem.at[1])
    load_g.start()

    def row_peer(dz, dc):
        return ((z + dz) % NZ) * 2 + (core + dc) % 2

    def view_peer(dx, dy):
        return ((x + dx) % XY) * XY + (y + dy) % XY

    barrier = pltpu.get_barrier_semaphore()
    for off in ROW_OFFS:
        pl.semaphore_signal(barrier, inc=1, device_id=(v, row_peer(*off)), device_id_type=MESH)
    for off in VIEW_OFFS:
        pl.semaphore_signal(barrier, inc=1, device_id=(view_peer(*off), r), device_id_type=MESH)

    row, col = iota((256, 256), 0), iota((256, 256), 1)
    pmat[...] = ((row // 16 == col % 16) & (row % 16 == col // 16)).astype(F32).astype(BF)

    load_x.wait()

    def permute(part):
        def pair(i, carry):
            a, b = 2 * i, 2 * i + 1
            blocks = [
                x_in[:, pl.ds(pl.multiple_of(t * ROWS + part * 16, 16), 16), :].reshape(256, 128) for t in (a, b)
            ]
            moved = jnp.dot(pmat[...], jnp.concatenate(blocks, axis=1), preferred_element_type=F32).astype(BF)
            for t, piece in ((a, moved[:, :128]), (b, moved[:, 128:])):
                zsrc[part * FOLD:(part + 1) * FOLD, t] = piece.reshape(FOLD, R * NV, 128)
            return carry

        lax.fori_loop(0, NR // 2, pair, 0)

    def send_rows(c):
        for off in ROW_OFFS:
            t = row_peer(*off)
            pltpu.make_async_remote_copy(
                src_ref=zsrc.at[c, t], dst_ref=zrecv.at[c, r], send_sem=z_send.at[c], recv_sem=z_recv.at[c],
                device_id=(v, t), device_id_type=MESH,
            ).start()
        pltpu.make_async_copy(zsrc.at[c, r], zrecv.at[c, r], z_recv.at[c]).start()

    permute(0)
    pl.semaphore_wait(barrier, len(ROW_OFFS) + len(VIEW_OFFS))
    for c in range(N // 2):
        send_rows(c)
    permute(1)
    for c in range(N // 2, N):
        send_rows(c)

    owners = [owner_ref[k] for k in range(NV)]
    ranks = []
    for k in range(NV):
        rank = jnp.int32(0)
        for j in range(k):
            rank = rank + jnp.where(owners[j] == owners[k], 1, 0).astype(I32)
        ranks.append(rank)
    slots = [owners[k] * 2 + ranks[k] for k in range(NV)]

    shape = (NV, 8, 128)
    slot_of = iota(shape, 0) * 2 + jnp.minimum(iota(shape, 1), 1)
    told = jnp.zeros(shape, F32)
    for k in range(NV):
        told = jnp.where(slot_of == slots[k], (fan_ref[k] + 1).astype(F32), told)
    msrc[...] = told
    for off in VIEW_OFFS:
        o = view_peer(*off)
        pltpu.make_async_remote_copy(
            src_ref=msrc.at[o], dst_ref=mrecv.at[v], send_sem=m_send, recv_sem=m_recv,
            device_id=(o, r), device_id_type=MESH,
        ).start()
    pltpu.make_async_copy(msrc.at[v], mrecv.at[v], m_recv).start()

    shape = (512, 256)
    row_slot = iota(shape, 0) // 16
    view_col = iota((8, 256), 1) % 16
    weights = jnp.zeros(shape, F32)
    for k in range(NV):
        band = jnp.where(
            view_col == start_ref[k], wt_ref[k, 0], jnp.where(view_col == start_ref[k] + 1, wt_ref[k, 1], 0.0)
        )
        weights = jnp.where(row_slot == slots[k], band[0:1, :], weights)
    same = iota(shape, 0) % 16 == iota(shape, 1) // 16
    wmat[...] = jnp.where(same, weights, 0.0).astype(BF)

    wait_for(mrecv, m_recv)
    lane_slot = iota((1, 128), 1) // 16
    for part in range(4):
        target = jnp.zeros((1, 128), F32)
        for s in range(4):
            for slot in range(2):
                target = jnp.where(lane_slot == 2 * s + slot, mrecv[4 * part + s, slot:slot + 1, :], target)
        shape = (256, 128)
        hit = (iota(shape, 0) // 16 + 1).astype(F32) == target
        same = iota(shape, 0) % 16 == iota(shape, 1) % 16
        cmat[:, 128 * part:128 * (part + 1)] = jnp.where(hit & same, 1.0, 0.0).astype(BF)

    load_g.wait()

    def collect(c):
        wait_for(fin.at[c], c_recv.at[c])
        raw[c] = jnp.dot(cmat[...], fin[c].reshape(512, L), preferred_element_type=F32)

    def step(c, carry):
        wait_for(zrecv.at[c], z_recv.at[c])
        lines = jnp.concatenate([zrecv[c, t] for t in range(NR)], axis=1)
        filtered = [
            jnp.dot(lines, g[C - 256 - 256 * j:2 * C - 256 - 256 * j, :], preferred_element_type=F32).astype(BF)
            for j in range(C // 256)
        ]
        per = L // 256
        folded = jnp.concatenate(
            [jnp.concatenate(filtered[q * per:(q + 1) * per], axis=1) for q in range(FOLD)], axis=0
        )
        contrib = jnp.dot(wmat[...], folded, preferred_element_type=F32).astype(BF)
        csrc[c] = contrib.reshape(NV, 32, L)
        for off in VIEW_OFFS:
            o = view_peer(*off)
            pltpu.make_async_remote_copy(
                src_ref=csrc.at[c, o], dst_ref=fin.at[c, v], send_sem=c_send.at[c], recv_sem=c_recv.at[c],
                device_id=(o, r), device_id_type=MESH,
            ).start()
        pltpu.make_async_copy(csrc.at[c, v], fin.at[c, v], c_recv.at[c]).start()

        @pl.when(c >= LAG)
        def _():
            collect(c - LAG)

        return carry

    lax.fori_loop(0, N, step, 0)
    for c in range(N - LAG, N):
        collect(c)

    for group in range(2):
        for q in range(FOLD):
            pieces = [
                raw[c].reshape(NV, 16, L)[:, R * q:R * (q + 1), :] for c in range(group * FOLD, (group + 1) * FOLD)
            ]
            whole = jnp.concatenate(pieces, axis=1)
            out_ref[:, 16 * group:16 * (group + 1), L * q:L * (q + 1)] = whole.astype(BF)

    wait_for(msrc.at[pl.ds(0, NV - 1)], m_send)

    def drain(c, carry):
        wait_for(zsrc.at[c, pl.ds(0, NR - 1)], z_send.at[c])
        wait_for(csrc.at[c, pl.ds(0, NV - 1)], c_send.at[c])
        return carry

    lax.fori_loop(0, N, drain, 0)


def on_device(grad_par, contrib_owner, contrib_fan, contrib_start, contrib_wt):
    smem = pl.BlockSpec(memory_space=pltpu.SMEM)
    anywhere = pl.BlockSpec(memory_space=pl.ANY)
    column = jnp.asarray(toeplitz_column())
    return pl.pallas_call(
        kernel,
        out_shape=jax.ShapeDtypeStruct((NV, ROWS, C), BF),
        in_specs=[smem, smem, smem, smem, anywhere, anywhere],
        out_specs=pl.BlockSpec(memory_space=pltpu.VMEM),
        scratch_shapes=[
            pltpu.VMEM((NV, 512, 128), BF),
            pltpu.VMEM((2 * C - 256, 256), BF),
            pltpu.VMEM((N, NR, R * NV, 128), BF),
            pltpu.VMEM((N, NR, R * NV, 128), BF),
            pltpu.VMEM((N, NV, 32, L), BF),
            pltpu.VMEM((N, NV, 32, L), BF),
            pltpu.VMEM((N, 256, L), F32),
            pltpu.VMEM((NV, 8, 128), F32),
            pltpu.VMEM((NV, 8, 128), F32),
            pltpu.VMEM((512, 256), BF),
            pltpu.VMEM((256, 512), BF),
            pltpu.VMEM((256, 256), BF),
            pltpu.SemaphoreType.DMA((2,)),
            pltpu.SemaphoreType.DMA((N,)),
            pltpu.SemaphoreType.DMA((N,)),
            pltpu.SemaphoreType.DMA((N,)),
            pltpu.SemaphoreType.DMA((N,)),
            pltpu.SemaphoreType.DMA,
            pltpu.SemaphoreType.DMA,
        ],
        compiler_params=pltpu.CompilerParams(
            collective_id=0, has_side_effects=True, vmem_limit_bytes=52 << 20
        ),
    )(contrib_owner[:, 0], contrib_fan, contrib_start, contrib_wt.astype(F32), grad_par, column)


def solution(mesh):
    return jax.shard_map(
        on_device,
        mesh=mesh,
        in_specs=(
            P("views", None, "rows"),
            P("views", None),
            P("views"),
            P("views"),
            P("views", None),
        ),
        out_specs=P("views", "rows", None),
        check_vma=False,
    )
```

```python
import functools
import math

import jax
import jax.numpy as jnp
import ml_dtypes
import numpy as np
from jax import lax
from jax.experimental import pallas as pl
from jax.experimental.pallas import tpu as pltpu
from jax.sharding import PartitionSpec as P

MESH = pl.DeviceIdType.MESH
BF = jnp.bfloat16
F32 = jnp.float32
I32 = jnp.int32

C = 2048
NV = 16
NR = 16
ROWS = 32
R = 4
N = ROWS // R
FOLD = 16 // R
L = C // FOLD
XY = 4
NZ = 8
LAG = 2

VIEW_OFFS = [(1, 0), (0, 1), (3, 0), (0, 3), (1, 1), (3, 3), (1, 3), (3, 1), (2, 0), (0, 2), (2, 1), (1, 2), (2, 3), (3, 2), (2, 2)]
ROW_OFFS = [(z, c) for z in (1, 7, 2, 6, 3, 5, 4) for c in (0, 1)] + [(0, 1)]


def toeplitz_column():
    m = np.arange(2 * C - 256)[:, None] - np.arange(256)[None, :] - (C - 256)
    distance = np.abs(m)
    far = np.maximum(distance.astype(np.float32), np.float32(1.0))
    odd = np.float32(-4.0) / (np.float32(math.pi**2) * far * far)
    values = np.where(distance == 0, np.float32(1.0), np.where(distance % 2 == 1, odd, np.float32(0.0)))
    return values.astype(ml_dtypes.bfloat16)


def iota(shape, dim):
    return lax.broadcasted_iota(I32, shape, dim)


def wait_for(ref, sem):
    pltpu.make_async_copy(ref, ref, sem).wait()


def kernel(owner_hbm, fan_hbm, start_hbm, wt_hbm, x_hbm, g_hbm, out_ref,
           owner_ref, fan_ref, start_ref, wt_ref, x_in, g, zsrc, zrecv, csrc, fin, raw, msrc, mrecv, wmat, cmat, pmat,
           in_sem, z_send, z_recv, c_send, c_recv, m_send, m_recv):
    v = lax.axis_index("views")
    r = lax.axis_index("rows")
    x, y = v // XY, v % XY
    z, core = r // 2, r % 2

    load_x = [
        pltpu.make_async_copy(
            x_hbm.at[:, 4 * ROWS * i:4 * ROWS * (i + 1), :], x_in.at[:, 4 * ROWS * i:4 * ROWS * (i + 1), :], in_sem.at[i]
        )
        for i in range(4)
    ]
    load_small = [
        pltpu.make_async_copy(src, dst, in_sem.at[5 + i])
        for i, (src, dst) in enumerate(
            ((owner_hbm, owner_ref), (fan_hbm, fan_ref), (start_hbm, start_ref), (wt_hbm, wt_ref))
        )
    ]
    load_g = pltpu.make_async_copy(g_hbm, g, in_sem.at[4])
    for copy in load_x + load_small + [load_g]:
        copy.start()

    def row_peer(dz, dc):
        return ((z + dz) % NZ) * 2 + (core + dc) % 2

    def view_peer(dx, dy):
        return ((x + dx) % XY) * XY + (y + dy) % XY

    barrier = pltpu.get_barrier_semaphore()
    for off in ROW_OFFS:
        pl.semaphore_signal(barrier, inc=1, device_id=(v, row_peer(*off)), device_id_type=MESH)
    for off in VIEW_OFFS:
        pl.semaphore_signal(barrier, inc=1, device_id=(view_peer(*off), r), device_id_type=MESH)

    row, col = iota((256, 256), 0), iota((256, 256), 1)
    pmat[...] = ((row // 16 == col % 16) & (row % 16 == col // 16)).astype(F32).astype(BF)

    def permute(part):
        for i in range(NR // 2):
            if part == 0 and i % 2 == 0:
                load_x[i // 2].wait()
            pair = (2 * i, 2 * i + 1)
            blocks = [x_in[:, t * ROWS + part * 16:t * ROWS + part * 16 + 16, :].reshape(256, 128) for t in pair]
            moved = jnp.dot(pmat[...], jnp.concatenate(blocks, axis=1), preferred_element_type=F32).astype(BF)
            for t, piece in zip(pair, (moved[:, :128], moved[:, 128:])):
                zsrc[part * FOLD:(part + 1) * FOLD, t] = piece.reshape(FOLD, R * NV, 128)

    def send_rows(c):
        for off in ROW_OFFS:
            t = row_peer(*off)
            pltpu.make_async_remote_copy(
                src_ref=zsrc.at[c, t], dst_ref=zrecv.at[c, r], send_sem=z_send.at[c], recv_sem=z_recv.at[c],
                device_id=(v, t), device_id_type=MESH,
            ).start()
        pltpu.make_async_copy(zsrc.at[c, r], zrecv.at[c, r], z_recv.at[c]).start()

    permute(0)
    pl.semaphore_wait(barrier, len(ROW_OFFS) + len(VIEW_OFFS))
    for c in range(N // 2):
        send_rows(c)
    permute(1)
    for c in range(N // 2, N):
        send_rows(c)

    for copy in load_small:
        copy.wait()
    owners = [owner_ref[k] for k in range(NV)]
    ranks = []
    for k in range(NV):
        rank = jnp.int32(0)
        for j in range(k):
            rank = rank + jnp.where(owners[j] == owners[k], 1, 0).astype(I32)
        ranks.append(rank)
    slots = [owners[k] * 2 + ranks[k] for k in range(NV)]

    shape = (NV, 8, 128)
    slot_of = iota(shape, 0) * 2 + jnp.minimum(iota(shape, 1), 1)
    told = jnp.zeros(shape, F32)
    for k in range(NV):
        told = jnp.where(slot_of == slots[k], (fan_ref[k] + 1).astype(F32), told)
    msrc[...] = told
    for off in VIEW_OFFS:
        o = view_peer(*off)
        pltpu.make_async_remote_copy(
            src_ref=msrc.at[o], dst_ref=mrecv.at[v], send_sem=m_send, recv_sem=m_recv,
            device_id=(o, r), device_id_type=MESH,
        ).start()
    pltpu.make_async_copy(msrc.at[v], mrecv.at[v], m_recv).start()

    shape = (512, 256)
    row_slot = iota(shape, 0) // 16
    view_col = iota((8, 256), 1) % 16
    wt = wt_ref[...].astype(F32)
    weights = jnp.zeros(shape, F32)
    for k in range(NV):
        band = jnp.where(
            view_col == start_ref[k], wt[0:1, k:k + 1],
            jnp.where(view_col == start_ref[k] + 1, wt[1:2, k:k + 1], 0.0),
        )
        weights = jnp.where(row_slot == slots[k], band[0:1, :], weights)
    same = iota(shape, 0) % 16 == iota(shape, 1) // 16
    wmat[...] = jnp.where(same, weights, 0.0).astype(BF)

    wait_for(mrecv, m_recv)
    lane_slot = iota((1, 128), 1) // 16
    for part in range(4):
        target = jnp.zeros((1, 128), F32)
        for s in range(4):
            for slot in range(2):
                target = jnp.where(lane_slot == 2 * s + slot, mrecv[4 * part + s, slot:slot + 1, :], target)
        shape = (256, 128)
        hit = (iota(shape, 0) // 16 + 1).astype(F32) == target
        same = iota(shape, 0) % 16 == iota(shape, 1) % 16
        cmat[:, 128 * part:128 * (part + 1)] = jnp.where(hit & same, 1.0, 0.0).astype(BF)

    load_g.wait()

    def collect(c):
        wait_for(fin.at[c], c_recv.at[c])
        raw[c] = jnp.dot(cmat[...], fin[c].reshape(512, L), preferred_element_type=F32)

    def step(c, carry):
        wait_for(zrecv.at[c], z_recv.at[c])
        lines = jnp.concatenate([zrecv[c, t] for t in range(NR)], axis=1)
        filtered = [
            jnp.dot(lines, g[C - 256 - 256 * j:2 * C - 256 - 256 * j, :], preferred_element_type=F32).astype(BF)
            for j in range(C // 256)
        ]
        per = L // 256
        folded = jnp.concatenate(
            [jnp.concatenate(filtered[q * per:(q + 1) * per], axis=1) for q in range(FOLD)], axis=0
        )
        contrib = jnp.dot(wmat[...], folded, preferred_element_type=F32).astype(BF)
        csrc[c] = contrib.reshape(NV, 32, L)
        for off in VIEW_OFFS:
            o = view_peer(*off)
            pltpu.make_async_remote_copy(
                src_ref=csrc.at[c, o], dst_ref=fin.at[c, v], send_sem=c_send.at[c], recv_sem=c_recv.at[c],
                device_id=(o, r), device_id_type=MESH,
            ).start()
        pltpu.make_async_copy(csrc.at[c, v], fin.at[c, v], c_recv.at[c]).start()

        @pl.when(c >= LAG)
        def _():
            collect(c - LAG)

        return carry

    lax.fori_loop(0, N, step, 0)
    def unfold(group):
        for q in range(FOLD):
            pieces = [
                raw[c].reshape(NV, 16, L)[:, R * q:R * (q + 1), :] for c in range(group * FOLD, (group + 1) * FOLD)
            ]
            whole = jnp.concatenate(pieces, axis=1)
            out_ref[:, 16 * group:16 * (group + 1), L * q:L * (q + 1)] = whole.astype(BF)

    unfold(0)
    for c in range(N - LAG, N):
        collect(c)
    unfold(1)

    wait_for(msrc.at[pl.ds(0, NV - 1)], m_send)

    def drain(c, carry):
        wait_for(zsrc.at[c, pl.ds(0, NR - 1)], z_send.at[c])
        wait_for(csrc.at[c, pl.ds(0, NV - 1)], c_send.at[c])
        return carry

    lax.fori_loop(0, N, drain, 0)


def on_device(grad_par, contrib_owner, contrib_fan, contrib_start, contrib_wt):
    hbm = pl.BlockSpec(memory_space=pltpu.HBM)
    vmem = pl.BlockSpec(memory_space=pltpu.VMEM)
    column = jnp.asarray(toeplitz_column())
    result = pl.pallas_call(
        kernel,
        out_shape=pltpu.VMEM((NV, ROWS, C), BF),
        in_specs=[hbm] * 6,
        out_specs=vmem,
        scratch_shapes=[
            pltpu.SMEM((NV,), I32),
            pltpu.SMEM((NV,), I32),
            pltpu.SMEM((NV,), I32),
            pltpu.VMEM((2, NV), BF),
            pltpu.VMEM((NV, 512, 128), BF),
            pltpu.VMEM((2 * C - 256, 256), BF),
            pltpu.VMEM((N, NR, R * NV, 128), BF),
            pltpu.VMEM((N, NR, R * NV, 128), BF),
            pltpu.VMEM((N, NV, 32, L), BF),
            pltpu.VMEM((N, NV, 32, L), BF),
            pltpu.VMEM((N, 256, L), F32),
            pltpu.VMEM((NV, 8, 128), F32),
            pltpu.VMEM((NV, 8, 128), F32),
            pltpu.VMEM((512, 256), BF),
            pltpu.VMEM((256, 512), BF),
            pltpu.VMEM((256, 256), BF),
            pltpu.SemaphoreType.DMA((9,)),
            pltpu.SemaphoreType.DMA((N,)),
            pltpu.SemaphoreType.DMA((N,)),
            pltpu.SemaphoreType.DMA((N,)),
            pltpu.SemaphoreType.DMA((N,)),
            pltpu.SemaphoreType.DMA,
            pltpu.SemaphoreType.DMA,
        ],
        compiler_params=pltpu.CompilerParams(
            collective_id=0, has_side_effects=True, vmem_limit_bytes=61 << 20
        ),
    )(contrib_owner[:, 0], contrib_fan, contrib_start, contrib_wt.T, grad_par, column)
    return result


def solution(mesh):
    return jax.shard_map(
        on_device,
        mesh=mesh,
        in_specs=(
            P("views", None, "rows"),
            P("views", None),
            P("views"),
            P("views"),
            P("views", None),
        ),
        out_specs=P("views", "rows", None),
        check_vma=False,
    )
```

```python
import functools
import math

import jax
import jax.numpy as jnp
import ml_dtypes
import numpy as np
from jax import lax
from jax.experimental import pallas as pl
from jax.experimental.pallas import tpu as pltpu
from jax.sharding import PartitionSpec as P

MESH = pl.DeviceIdType.MESH
BF = jnp.bfloat16
F32 = jnp.float32
I32 = jnp.int32

C = 2048
NV = 16
NR = 16
ROWS = 32
R = 2
N = ROWS // R
FOLD = 16 // R
L = C // FOLD
XY = 4
NZ = 8
LAG = 4
AHEAD = 6

VIEW_OFFS = [(1, 0), (0, 1), (3, 0), (0, 3), (1, 1), (3, 3), (1, 3), (3, 1), (2, 0), (0, 2), (2, 1), (1, 2), (2, 3), (3, 2), (2, 2)]
ROW_OFFS = [(z, c) for z in (1, 7, 2, 6, 3, 5, 4) for c in (0, 1)] + [(0, 1)]


def toeplitz_column():
    m = np.arange(2 * C - 256)[:, None] - np.arange(256)[None, :] - (C - 256)
    distance = np.abs(m)
    far = np.maximum(distance.astype(np.float32), np.float32(1.0))
    odd = np.float32(-4.0) / (np.float32(math.pi**2) * far * far)
    values = np.where(distance == 0, np.float32(1.0), np.where(distance % 2 == 1, odd, np.float32(0.0)))
    return values.astype(ml_dtypes.bfloat16)


def iota(shape, dim):
    return lax.broadcasted_iota(I32, shape, dim)


def wait_for(ref, sem):
    pltpu.make_async_copy(ref, ref, sem).wait()


def kernel(owner_hbm, fan_hbm, start_hbm, wt_hbm, x_hbm, g_hbm, out_ref,
           owner_ref, fan_ref, start_ref, wt_ref, x_in, g, zsrc, zrecv, csrc, fin, raw, msrc, mrecv, wmat, cmat, pmat,
           in_sem, z_send, z_recv, c_send, c_recv, m_send, m_recv):
    v = lax.axis_index("views")
    r = lax.axis_index("rows")
    x, y = v // XY, v % XY
    z, core = r // 2, r % 2

    load_x = [
        pltpu.make_async_copy(
            x_hbm.at[:, 4 * ROWS * i:4 * ROWS * (i + 1), :], x_in.at[:, 4 * ROWS * i:4 * ROWS * (i + 1), :], in_sem.at[i]
        )
        for i in range(4)
    ]
    load_small = [
        pltpu.make_async_copy(src, dst, in_sem.at[5 + i])
        for i, (src, dst) in enumerate(
            ((owner_hbm, owner_ref), (fan_hbm, fan_ref), (start_hbm, start_ref), (wt_hbm, wt_ref))
        )
    ]
    load_g = pltpu.make_async_copy(g_hbm, g, in_sem.at[4])
    for copy in load_x + load_small + [load_g]:
        copy.start()

    def row_peer(dz, dc):
        return ((z + dz) % NZ) * 2 + (core + dc) % 2

    def view_peer(dx, dy):
        return ((x + dx) % XY) * XY + (y + dy) % XY

    row_peers = [row_peer(*off) for off in ROW_OFFS]
    view_peers = [view_peer(*off) for off in VIEW_OFFS]

    barrier = pltpu.get_barrier_semaphore()
    for t in row_peers:
        pl.semaphore_signal(barrier, inc=1, device_id=(v, t), device_id_type=MESH)
    for o in view_peers:
        pl.semaphore_signal(barrier, inc=1, device_id=(o, r), device_id_type=MESH)

    row, col = iota((256, 256), 0), iota((256, 256), 1)
    pmat[...] = ((row // 16 == col % 16) & (row % 16 == col // 16)).astype(F32).astype(BF)

    def permute(part):
        for i in range(NR // 2):
            if part == 0 and i % 2 == 0:
                load_x[i // 2].wait()
            pair = (2 * i, 2 * i + 1)
            blocks = [x_in[:, t * ROWS + part * 16:t * ROWS + part * 16 + 16, :].reshape(256, 128) for t in pair]
            moved = jnp.dot(pmat[...], jnp.concatenate(blocks, axis=1), preferred_element_type=F32).astype(BF)
            for t, piece in zip(pair, (moved[:, :128], moved[:, 128:])):
                zsrc[part * FOLD:(part + 1) * FOLD, t] = piece.reshape(FOLD, R * NV, 128)

    def send_rows(c):
        for t in row_peers:
            pltpu.make_async_remote_copy(
                src_ref=zsrc.at[c, t], dst_ref=zrecv.at[c, r], send_sem=z_send.at[c], recv_sem=z_recv.at[c],
                device_id=(v, t), device_id_type=MESH,
            ).start()
        pltpu.make_async_copy(zsrc.at[c, r], zrecv.at[c, r], z_recv.at[c]).start()

    permute(0)
    pl.semaphore_wait(barrier, len(ROW_OFFS) + len(VIEW_OFFS))
    for c in range(AHEAD):
        send_rows(c)

    for copy in load_small:
        copy.wait()
    owners = [owner_ref[k] for k in range(NV)]
    ranks = []
    for k in range(NV):
        rank = jnp.int32(0)
        for j in range(k):
            rank = rank + jnp.where(owners[j] == owners[k], 1, 0).astype(I32)
        ranks.append(rank)
    slots = [owners[k] * 2 + ranks[k] for k in range(NV)]

    shape = (NV, 8, 128)
    slot_of = iota(shape, 0) * 2 + jnp.minimum(iota(shape, 1), 1)
    told = jnp.zeros(shape, F32)
    for k in range(NV):
        told = jnp.where(slot_of == slots[k], (fan_ref[k] + 1).astype(F32), told)
    msrc[...] = told
    for o in view_peers:
        pltpu.make_async_remote_copy(
            src_ref=msrc.at[o], dst_ref=mrecv.at[v], send_sem=m_send, recv_sem=m_recv,
            device_id=(o, r), device_id_type=MESH,
        ).start()
    pltpu.make_async_copy(msrc.at[v], mrecv.at[v], m_recv).start()

    shape = (512, 256)
    row_slot = iota(shape, 0) // 16
    view_col = iota((8, 256), 1) % 16
    wt = wt_ref[...].astype(F32)
    weights = jnp.zeros(shape, F32)
    for k in range(NV):
        band = jnp.where(
            view_col == start_ref[k], wt[0:1, k:k + 1],
            jnp.where(view_col == start_ref[k] + 1, wt[1:2, k:k + 1], 0.0),
        )
        weights = jnp.where(row_slot == slots[k], band[0:1, :], weights)
    same = iota(shape, 0) % 16 == iota(shape, 1) // 16
    wmat[...] = jnp.where(same, weights, 0.0).astype(BF)

    load_g.wait()

    def collect(c):
        wait_for(fin.at[c], c_recv.at[c])
        raw[c] = jnp.dot(cmat[...], fin[c].reshape(512, L), preferred_element_type=F32)

    def build_sum():
        wait_for(mrecv, m_recv)
        lane_slot = iota((1, 128), 1) // 16
        for part in range(4):
            target = jnp.zeros((1, 128), F32)
            for s in range(4):
                for slot in range(2):
                    target = jnp.where(lane_slot == 2 * s + slot, mrecv[4 * part + s, slot:slot + 1, :], target)
            shape = (256, 128)
            hit = (iota(shape, 0) // 16 + 1).astype(F32) == target
            same = iota(shape, 0) % 16 == iota(shape, 1) % 16
            cmat[:, 128 * part:128 * (part + 1)] = jnp.where(hit & same, 1.0, 0.0).astype(BF)

    def step(c, ahead, behind):
        wait_for(zrecv.at[c], z_recv.at[c])
        lines = jnp.concatenate([zrecv[c, t] for t in range(NR)], axis=1)
        filtered = [
            jnp.dot(lines, g[C - 256 - 256 * j:2 * C - 256 - 256 * j, :], preferred_element_type=F32).astype(BF)
            for j in range(C // 256)
        ]
        per = L // 256
        folded = jnp.concatenate(
            [jnp.concatenate(filtered[q * per:(q + 1) * per], axis=1) for q in range(FOLD)], axis=0
        )
        contrib = jnp.dot(wmat[...], folded, preferred_element_type=F32).astype(BF)
        csrc[c] = contrib.reshape(NV, 32, L)
        for o in view_peers:
            pltpu.make_async_remote_copy(
                src_ref=csrc.at[c, o], dst_ref=fin.at[c, v], send_sem=c_send.at[c], recv_sem=c_recv.at[c],
                device_id=(o, r), device_id_type=MESH,
            ).start()
        pltpu.make_async_copy(csrc.at[c, v], fin.at[c, v], c_recv.at[c]).start()
        if ahead:
            send_rows(c + AHEAD)
        if behind:
            collect(c - LAG)

    def steps(first, last, ahead, behind):
        def body(c, carry):
            step(c, ahead, behind)
            return carry

        lax.fori_loop(first, last, body, 0)

    turns = sorted({0, N // 2 - AHEAD, LAG, N - AHEAD, N})
    for first, last in zip(turns, turns[1:]):
        if first == N // 2 - AHEAD:
            permute(1)
        if first == LAG:
            build_sum()
        steps(first, last, first < N - AHEAD, first >= LAG)

    def unfold(group):
        for q in range(FOLD):
            pieces = [
                raw[c].reshape(NV, 16, L)[:, R * q:R * (q + 1), :] for c in range(group * FOLD, (group + 1) * FOLD)
            ]
            whole = jnp.concatenate(pieces, axis=1)
            out_ref[:, 16 * group:16 * (group + 1), L * q:L * (q + 1)] = whole.astype(BF)

    unfold(0)
    for c in range(N - LAG, N):
        collect(c)
    unfold(1)

    wait_for(msrc.at[pl.ds(0, NV - 1)], m_send)

    def drain(c, carry):
        wait_for(zsrc.at[c, pl.ds(0, NR - 1)], z_send.at[c])
        wait_for(csrc.at[c, pl.ds(0, NV - 1)], c_send.at[c])
        return carry

    lax.fori_loop(0, N, drain, 0)


def on_device(grad_par, contrib_owner, contrib_fan, contrib_start, contrib_wt):
    hbm = pl.BlockSpec(memory_space=pltpu.HBM)
    vmem = pl.BlockSpec(memory_space=pltpu.VMEM)
    column = jnp.asarray(toeplitz_column())
    result = pl.pallas_call(
        kernel,
        out_shape=pltpu.VMEM((NV, ROWS, C), BF),
        in_specs=[hbm] * 6,
        out_specs=vmem,
        scratch_shapes=[
            pltpu.SMEM((NV,), I32),
            pltpu.SMEM((NV,), I32),
            pltpu.SMEM((NV,), I32),
            pltpu.VMEM((2, NV), BF),
            pltpu.VMEM((NV, 512, 128), BF),
            pltpu.VMEM((2 * C - 256, 256), BF),
            pltpu.VMEM((N, NR, R * NV, 128), BF),
            pltpu.VMEM((N, NR, R * NV, 128), BF),
            pltpu.VMEM((N, NV, 32, L), BF),
            pltpu.VMEM((N, NV, 32, L), BF),
            pltpu.VMEM((N, 256, L), F32),
            pltpu.VMEM((NV, 8, 128), F32),
            pltpu.VMEM((NV, 8, 128), F32),
            pltpu.VMEM((512, 256), BF),
            pltpu.VMEM((256, 512), BF),
            pltpu.VMEM((256, 256), BF),
            pltpu.SemaphoreType.DMA((9,)),
            pltpu.SemaphoreType.DMA((N,)),
            pltpu.SemaphoreType.DMA((N,)),
            pltpu.SemaphoreType.DMA((N,)),
            pltpu.SemaphoreType.DMA((N,)),
            pltpu.SemaphoreType.DMA,
            pltpu.SemaphoreType.DMA,
        ],
        compiler_params=pltpu.CompilerParams(
            collective_id=0, has_side_effects=True, vmem_limit_bytes=61 << 20
        ),
    )(contrib_owner[:, 0], contrib_fan, contrib_start, contrib_wt.T, grad_par, column)
    return result


def solution(mesh):
    return jax.shard_map(
        on_device,
        mesh=mesh,
        in_specs=(
            P("views", None, "rows"),
            P("views", None),
            P("views"),
            P("views"),
            P("views", None),
        ),
        out_specs=P("views", "rows", None),
        check_vma=False,
    )
```

```python
import functools
import math

import jax
import jax.numpy as jnp
import ml_dtypes
import numpy as np
from jax import lax
from jax.experimental import pallas as pl
from jax.experimental.pallas import tpu as pltpu
from jax.sharding import PartitionSpec as P

MESH = pl.DeviceIdType.MESH
BF = jnp.bfloat16
F32 = jnp.float32
I32 = jnp.int32

C = 2048
NV = 16
NR = 16
ROWS = 32
R = 2
N = ROWS // R
FOLD = 16 // R
L = C // FOLD
XY = 4
NZ = 8
LAG = 4
AHEAD = 6

VIEW_OFFS = [(1, 0), (0, 1), (3, 0), (0, 3), (1, 1), (3, 3), (1, 3), (3, 1), (2, 0), (0, 2), (2, 1), (1, 2), (2, 3), (3, 2), (2, 2)]
ROW_OFFS = [(z, c) for z in (1, 7, 2, 6, 3, 5, 4) for c in (0, 1)] + [(0, 1)]


def toeplitz_column():
    m = np.arange(2 * C - 256)[:, None] - np.arange(256)[None, :] - (C - 256)
    distance = np.abs(m)
    far = np.maximum(distance.astype(np.float32), np.float32(1.0))
    odd = np.float32(-4.0) / (np.float32(math.pi**2) * far * far)
    values = np.where(distance == 0, np.float32(1.0), np.where(distance % 2 == 1, odd, np.float32(0.0)))
    return values.astype(ml_dtypes.bfloat16)


def iota(shape, dim):
    return lax.broadcasted_iota(I32, shape, dim)


def wait_for(ref, sem):
    pltpu.make_async_copy(ref, ref, sem).wait()


def kernel(owner_hbm, fan_hbm, start_hbm, wt_hbm, x_hbm, g_hbm, out_ref,
           owner_ref, fan_ref, start_ref, wt_ref, x_in, g, zsrc, zrecv, csrc, fin, raw, held, msrc, mrecv, wmat, cmat, pmat,
           in_sem, z_send, z_recv, c_send, c_recv, m_send, m_recv):
    v = lax.axis_index("views")
    r = lax.axis_index("rows")
    x, y = v // XY, v % XY
    z, core = r // 2, r % 2

    load_x = [
        pltpu.make_async_copy(
            x_hbm.at[:, 4 * ROWS * i:4 * ROWS * (i + 1), :], x_in.at[:, 4 * ROWS * i:4 * ROWS * (i + 1), :], in_sem.at[i]
        )
        for i in range(4)
    ]
    load_small = [
        pltpu.make_async_copy(src, dst, in_sem.at[5 + i])
        for i, (src, dst) in enumerate(
            ((owner_hbm, owner_ref), (fan_hbm, fan_ref), (start_hbm, start_ref), (wt_hbm, wt_ref))
        )
    ]
    load_g = pltpu.make_async_copy(g_hbm, g, in_sem.at[4])
    for copy in load_x + load_small + [load_g]:
        copy.start()

    def row_peer(dz, dc):
        return ((z + dz) % NZ) * 2 + (core + dc) % 2

    def view_peer(dx, dy):
        return ((x + dx) % XY) * XY + (y + dy) % XY

    row_peers = [row_peer(*off) for off in ROW_OFFS]
    view_peers = [view_peer(*off) for off in VIEW_OFFS]

    barrier = pltpu.get_barrier_semaphore()
    for t in row_peers:
        pl.semaphore_signal(barrier, inc=1, device_id=(v, t), device_id_type=MESH)
    for o in view_peers:
        pl.semaphore_signal(barrier, inc=1, device_id=(o, r), device_id_type=MESH)

    row, col = iota((256, 256), 0), iota((256, 256), 1)
    pmat[...] = ((row // 16 == col % 16) & (row % 16 == col // 16)).astype(F32).astype(BF)

    def permute(part):
        for i in range(NR // 2):
            if part == 0 and i % 2 == 0:
                load_x[i // 2].wait()
            pair = (2 * i, 2 * i + 1)
            blocks = [x_in[:, t * ROWS + part * 16:t * ROWS + part * 16 + 16, :].reshape(256, 128) for t in pair]
            moved = jnp.dot(pmat[...], jnp.concatenate(blocks, axis=1), preferred_element_type=F32).astype(BF)
            for t, piece in zip(pair, (moved[:, :128], moved[:, 128:])):
                zsrc[part * FOLD:(part + 1) * FOLD, t] = piece.reshape(FOLD, R * NV, 128)

    def send_rows(c):
        for t in row_peers:
            pltpu.make_async_remote_copy(
                src_ref=zsrc.at[c, t], dst_ref=zrecv.at[c, r], send_sem=z_send.at[c], recv_sem=z_recv.at[c],
                device_id=(v, t), device_id_type=MESH,
            ).start()
        pltpu.make_async_copy(zsrc.at[c, r], zrecv.at[c, r], z_recv.at[c]).start()

    permute(0)
    pl.semaphore_wait(barrier, len(ROW_OFFS) + len(VIEW_OFFS))
    for c in range(AHEAD):
        send_rows(c)

    for copy in load_small:
        copy.wait()
    owners = [owner_ref[k] for k in range(NV)]
    ranks = []
    for k in range(NV):
        rank = jnp.int32(0)
        for j in range(k):
            rank = rank + jnp.where(owners[j] == owners[k], 1, 0).astype(I32)
        ranks.append(rank)
    slots = [owners[k] * 2 + ranks[k] for k in range(NV)]

    shape = (NV, 8, 128)
    slot_of = iota(shape, 0) * 2 + jnp.minimum(iota(shape, 1), 1)
    told = jnp.zeros(shape, F32)
    for k in range(NV):
        told = jnp.where(slot_of == slots[k], (fan_ref[k] + 1).astype(F32), told)
    msrc[...] = told
    for o in view_peers:
        pltpu.make_async_remote_copy(
            src_ref=msrc.at[o], dst_ref=mrecv.at[v], send_sem=m_send, recv_sem=m_recv,
            device_id=(o, r), device_id_type=MESH,
        ).start()
    pltpu.make_async_copy(msrc.at[v], mrecv.at[v], m_recv).start()

    shape = (512, 256)
    row_slot = iota(shape, 0) // 16
    view_col = iota((8, 256), 1) % 16
    wt = wt_ref[...].astype(F32)
    weights = jnp.zeros(shape, F32)
    for k in range(NV):
        band = jnp.where(
            view_col == start_ref[k], wt[0:1, k:k + 1],
            jnp.where(view_col == start_ref[k] + 1, wt[1:2, k:k + 1], 0.0),
        )
        weights = jnp.where(row_slot == slots[k], band[0:1, :], weights)
    same = iota(shape, 0) % 16 == iota(shape, 1) // 16
    wmat[...] = jnp.where(same, weights, 0.0).astype(BF)

    load_g.wait()

    def collect(c):
        wait_for(fin.at[c], c_recv.at[c])
        raw[c] = jnp.dot(cmat[...], fin[c].reshape(512, L), preferred_element_type=F32)

    def build_sum():
        wait_for(mrecv, m_recv)
        lane_slot = iota((1, 128), 1) // 16
        for part in range(4):
            target = jnp.zeros((1, 128), F32)
            for s in range(4):
                for slot in range(2):
                    target = jnp.where(lane_slot == 2 * s + slot, mrecv[4 * part + s, slot:slot + 1, :], target)
            shape = (256, 128)
            hit = (iota(shape, 0) // 16 + 1).astype(F32) == target
            same = iota(shape, 0) % 16 == iota(shape, 1) % 16
            cmat[:, 128 * part:128 * (part + 1)] = jnp.where(hit & same, 1.0, 0.0).astype(BF)

    def step(c, ahead, behind):
        wait_for(zrecv.at[c], z_recv.at[c])
        lines = jnp.concatenate([zrecv[c, t] for t in range(NR)], axis=1)
        filtered = [
            jnp.dot(lines, g[C - 256 - 256 * j:2 * C - 256 - 256 * j, :], preferred_element_type=F32).astype(BF)
            for j in range(C // 256)
        ]
        per = L // 256
        folded = jnp.concatenate(
            [jnp.concatenate(filtered[q * per:(q + 1) * per], axis=1) for q in range(FOLD)], axis=0
        )
        contrib = jnp.dot(wmat[...], folded, preferred_element_type=F32).astype(BF)
        csrc[c] = contrib.reshape(NV, 32, L)
        for o in view_peers:
            pltpu.make_async_remote_copy(
                src_ref=csrc.at[c, o], dst_ref=fin.at[c, v], send_sem=c_send.at[c], recv_sem=c_recv.at[c],
                device_id=(o, r), device_id_type=MESH,
            ).start()
        pltpu.make_async_copy(csrc.at[c, v], fin.at[c, v], c_recv.at[c]).start()
        if ahead:
            send_rows(c + AHEAD)
        if behind:
            collect(c - LAG)

    def steps(first, last, ahead, behind):
        def body(c, carry):
            step(c, ahead, behind)
            return carry

        lax.fori_loop(first, last, body, 0)

    turns = sorted({0, N // 2 - AHEAD, LAG, N - AHEAD, N})
    for first, last in zip(turns, turns[1:]):
        if first == N // 2 - AHEAD:
            permute(1)
        if first == LAG:
            build_sum()
        steps(first, last, first < N - AHEAD, first >= LAG)

    def eight_rows(part, q):
        chunks = range(part * FOLD // 2, (part + 1) * FOLD // 2)
        return jnp.concatenate([raw[c].reshape(NV, 16, L)[:, R * q:R * (q + 1), :] for c in chunks], axis=1)

    blocks = [slice(L * q, L * (q + 1)) for q in range(FOLD)]
    for q in range(FOLD):
        whole = jnp.concatenate([eight_rows(0, q), eight_rows(1, q)], axis=1)
        out_ref[:, 0:16, blocks[q]] = whole.astype(BF)
    for q in range(FOLD):
        held[:, :, blocks[q]] = eight_rows(2, q)

    wait_for(msrc.at[pl.ds(0, NV - 1)], m_send)

    def drain(c, carry):
        wait_for(zsrc.at[c, pl.ds(0, NR - 1)], z_send.at[c])
        wait_for(csrc.at[c, pl.ds(0, NV - 1)], c_send.at[c])
        return carry

    lax.fori_loop(0, N - LAG, drain, 0)
    for c in range(N - LAG, N):
        collect(c)
    for q in range(FOLD):
        whole = jnp.concatenate([held[:, :, blocks[q]], eight_rows(3, q)], axis=1)
        out_ref[:, 16:32, blocks[q]] = whole.astype(BF)
    lax.fori_loop(N - LAG, N, drain, 0)


def on_device(grad_par, contrib_owner, contrib_fan, contrib_start, contrib_wt):
    hbm = pl.BlockSpec(memory_space=pltpu.HBM)
    vmem = pl.BlockSpec(memory_space=pltpu.VMEM)
    column = jnp.asarray(toeplitz_column())
    result = pl.pallas_call(
        kernel,
        out_shape=pltpu.VMEM((NV, ROWS, C), BF),
        in_specs=[hbm] * 6,
        out_specs=vmem,
        scratch_shapes=[
            pltpu.SMEM((NV,), I32),
            pltpu.SMEM((NV,), I32),
            pltpu.SMEM((NV,), I32),
            pltpu.VMEM((2, NV), BF),
            pltpu.VMEM((NV, 512, 128), BF),
            pltpu.VMEM((2 * C - 256, 256), BF),
            pltpu.VMEM((N, NR, R * NV, 128), BF),
            pltpu.VMEM((N, NR, R * NV, 128), BF),
            pltpu.VMEM((N, NV, 32, L), BF),
            pltpu.VMEM((N, NV, 32, L), BF),
            pltpu.VMEM((N, 256, L), F32),
            pltpu.VMEM((NV, 8, C), F32),
            pltpu.VMEM((NV, 8, 128), F32),
            pltpu.VMEM((NV, 8, 128), F32),
            pltpu.VMEM((512, 256), BF),
            pltpu.VMEM((256, 512), BF),
            pltpu.VMEM((256, 256), BF),
            pltpu.SemaphoreType.DMA((9,)),
            pltpu.SemaphoreType.DMA((N,)),
            pltpu.SemaphoreType.DMA((N,)),
            pltpu.SemaphoreType.DMA((N,)),
            pltpu.SemaphoreType.DMA((N,)),
            pltpu.SemaphoreType.DMA,
            pltpu.SemaphoreType.DMA,
        ],
        compiler_params=pltpu.CompilerParams(
            collective_id=0, has_side_effects=True, vmem_limit_bytes=61 << 20
        ),
    )(contrib_owner[:, 0], contrib_fan, contrib_start, contrib_wt.T, grad_par, column)
    return result


def solution(mesh):
    return jax.shard_map(
        on_device,
        mesh=mesh,
        in_specs=(
            P("views", None, "rows"),
            P("views", None),
            P("views"),
            P("views"),
            P("views", None),
        ),
        out_specs=P("views", "rows", None),
        check_vma=False,
    )
```
